32 devices in a mesh: seq: 4 (over z), guid: 2 (over core), tp: 4 (over y, x).
Axes of the slice: x: 2, y: 2, z: 4, core: 2. Of those that a mesh axis runs over, the one named last changes fastest.
Arguments:
- hidden_states: bfloat16 [2, 1536, 3072], P('guid', 'seq'), may hold values from -6 to 6
- modulation: float32 [2, 3, 3072], P('guid')
- w_query: bfloat16 [3072, 3072], P(None, 'tp'), may hold values from -0.109375 to 0.109375
- w_key: bfloat16 [3072, 3072], P(None, 'tp'), may hold values from -0.109375 to 0.109375
- w_value: bfloat16 [3072, 3072], P(None, 'tp'), may hold values from -0.109375 to 0.109375
- w_out: bfloat16 [3072, 3072], P('tp'), may hold values from -0.109375 to 0.109375
- block_ids: int32 [12, 7], P('seq'), may hold values from 0 to 11, as said below
- block_count: int32 [12], P('seq'), may hold values from 1 to 7, as said below
- guidance: float32 [1], replicated, may hold values from 4 to 8
Outputs:
- guided: bfloat16 [1536, 3072], P('seq', ('guid', 'tp'))
The draws below stay inside these ranges and needn't reach their ends.
Inputs may be any that keep to these rules, and one draw needn't show every extreme that they name: `block_ids`: entry 0 of each list is the query tile itself; the first block_count entries are distinct tiles within 3 tiles of the query tile; later entries repeat the query tile. `block_count`: some query tile lists 7 tiles.
All inputs are finite; a program needn't handle non-finite values.
Results may differ from the reference program's by a relative error of at most 0.02.
The reference program's roundings to bfloat16 on the way count: a program that leaves them out, or rounds other values in their place, can miss the bound.
Values may be sent and summed in bfloat16 or wider, within the bound.
No kernel may reach another device: no remote copies, remote signals or barrier semaphores. Data moves between devices by JAX's collectives and lax.ppermute only.
A program may use at most 192 MiB of HBM per device.

```python
import jax
import jax.numpy as jnp
from jax import lax

D = 3072
HEADS = 48
HD = 64
TILE = 128
TOKENS = 1536
TILES = 12
REACH = 3
KMAX = 7


def mask_tables(key):
    base = jax.random.fold_in(key, 7)
    first_key, second_key = jax.random.split(base, 2)
    span = 2 * REACH + 1
    offsets = jnp.arange(span, dtype=jnp.int32) - REACH
    row_keys = jax.random.split(first_key, TILES)
    ranks = jax.vmap(lambda one: jax.random.permutation(one, span))(row_keys).astype(jnp.int32)
    rows = jnp.arange(TILES, dtype=jnp.int32)
    index = rows[:, None] + offsets[None, :]
    valid = (index >= 0) & (index < TILES)
    order_key = jnp.where(offsets[None, :] == 0, -1, jnp.where(valid, ranks, ranks + span))
    order = jnp.argsort(order_key, axis=1, stable=True)
    picked = jnp.take_along_axis(index, order, axis=1)[:, :KMAX]
    counted = jax.random.randint(second_key, (TILES,), 1, KMAX + 1).astype(jnp.int32)
    counted = jnp.minimum(counted, jnp.sum(valid.astype(jnp.int32), axis=1))
    counted = jnp.where(rows == TILES // 2, KMAX, counted).astype(jnp.int32)
    slots = jnp.arange(KMAX, dtype=jnp.int32)[None, :]
    listed = jnp.where(slots < counted[:, None], picked, rows[:, None]).astype(jnp.int32)
    return (listed, counted)


def draw_block_ids(key, part):
    return mask_tables(key)[0]


def draw_block_count(key, part):
    return mask_tables(key)[1]


def draw_modulation(key, part):
    base = jax.random.fold_in(key, 11)
    k_shift, k_scale, k_gate = jax.random.split(base, 3)
    shift = 0.5 * jax.random.normal(k_shift, (2, D), jnp.float32)
    gate = 1.0 + 0.5 * jax.random.normal(k_gate, (2, D), jnp.float32)
    scale = 0.5 * jax.random.normal(k_scale, (2, D), jnp.float32)
    return jnp.stack([shift, scale, gate], axis=1).astype(jnp.float32)


def level_of(own_key, dims, pieces, least, top_value):
    def one(position, parts):
        heights = jax.random.uniform(jax.random.fold_in(jax.random.fold_in(own_key, 6), position), (parts,), jnp.float32, least / len(pieces), top_value / len(pieces))
        return jnp.repeat(jnp.exp(heights), dims[position] // parts).reshape((-1,) + (1,) * (len(dims) - position - 1))

    level = one(*pieces[0])
    for cut in pieces[1:]:
        level = level * one(*cut)
    return level


def gaussian(rng, extent, scale, limit, shards=(), kind=jnp.bfloat16):
    values = scale * jax.random.normal(rng, extent, jnp.float32)
    if shards:
        values = values * level_of(rng, extent, shards, -0.22, 0.18)
    return jnp.clip(values, -limit, limit).astype(kind)


def setup_inputs(seed: int = 0) -> dict:
    arg_keys = jax.random.split(jax.random.key(seed), 10)
    return {
        "hidden_states": gaussian(arg_keys[0], (2, TOKENS, D), 1.0, 6.0, ((0, 2), (1, 4))),
        "modulation": draw_modulation(jax.random.fold_in(arg_keys[9], 71), 0),
        "w_query": gaussian(arg_keys[2], (D, HEADS * HD), D ** -0.5, 0.109375, ((1, 4),)),
        "w_key": gaussian(arg_keys[3], (D, HEADS * HD), D ** -0.5, 0.109375, ((1, 4),)),
        "w_value": gaussian(arg_keys[4], (D, HEADS * HD), D ** -0.5, 0.109375, ((1, 4),)),
        "w_out": gaussian(arg_keys[5], (HEADS * HD, D), (HEADS * HD) ** -0.5, 0.109375, ((0, 4),)),
        "block_ids": draw_block_ids(jax.random.fold_in(arg_keys[9], 71), 0),
        "block_count": draw_block_count(jax.random.fold_in(arg_keys[9], 71), 0),
        "guidance": jnp.clip(jax.random.uniform(arg_keys[8], (1,), jnp.float32, 4.0, 8.0), 4.0, 8.0),
    }


def tile_table(block_ids, block_count):
    live = jnp.arange(block_ids.shape[1], dtype=jnp.int32)[None, :] < block_count[:, None]
    every = jnp.arange(TILES, dtype=jnp.int32)
    hit = (block_ids[:, :, None] == every[None, None, :]) & live[:, :, None]
    return jnp.any(hit, axis=1).astype(jnp.int32)

def one_branch(states, modul, w_query, w_key, w_value, w_out, allowed):
    xf = states.astype(jnp.float32)
    mean = lax.optimization_barrier(jnp.mean(xf, axis=1, keepdims=True))
    var = lax.optimization_barrier(jnp.mean((xf - mean) ** 2, axis=1, keepdims=True))
    normed = (xf - mean) / jnp.sqrt(var + 1e-05)
    h = (normed * (1.0 + modul[1]) + modul[0]).astype(jnp.bfloat16)
    query = lax.optimization_barrier(jnp.dot(h, w_query, preferred_element_type=jnp.float32).astype(jnp.bfloat16)).astype(jnp.float32)
    keys = lax.optimization_barrier(jnp.dot(h, w_key, preferred_element_type=jnp.float32).astype(jnp.bfloat16)).astype(jnp.float32)
    values = lax.optimization_barrier(jnp.dot(h, w_value, preferred_element_type=jnp.float32).astype(jnp.bfloat16)).astype(jnp.float32)
    span = min(2 * REACH + 1, TILES)

    def one_tile(tile_idx):
        rows = lax.dynamic_slice_in_dim(query, tile_idx * TILE, TILE, 0).reshape(TILE, HEADS, HD)
        first = jnp.clip(tile_idx - REACH, 0, TILES - span).astype(jnp.int32)
        near_k = lax.dynamic_slice_in_dim(keys, first * TILE, span * TILE, 0).reshape(span * TILE, HEADS, HD)
        near_v = lax.dynamic_slice_in_dim(values, first * TILE, span * TILE, 0).reshape(span * TILE, HEADS, HD)
        tile_ok = lax.dynamic_slice_in_dim(allowed[tile_idx], first, span, 0) > 0
        mask = jnp.repeat(tile_ok, TILE)[None, None, :]
        scores = jnp.einsum('qhd,khd->hqk', rows, near_k) * 0.125
        scores = jnp.where(mask, scores, -1e+30)
        top = lax.optimization_barrier(jnp.max(scores, axis=2, keepdims=True))
        expo = jnp.where(mask, jnp.exp(scores - top), 0.0)
        total = lax.optimization_barrier(jnp.sum(expo, axis=2))
        rounded = lax.optimization_barrier(expo.astype(jnp.bfloat16)).astype(jnp.float32)
        summed = jnp.einsum('hqk,khd->qhd', rounded, near_v)
        result = summed / jnp.transpose(total)[:, :, None]
        return result.reshape(TILE, HEADS * HD).astype(jnp.bfloat16)
    attn = lax.map(one_tile, jnp.arange(TILES, dtype=jnp.int32)).reshape(TOKENS, HEADS * HD)
    proj = jnp.dot(attn, w_out, preferred_element_type=jnp.float32)
    return xf + modul[2] * proj

def reference(hidden_states, modulation, w_query, w_key, w_value, w_out, block_ids, block_count, guidance):
    allowed = tile_table(block_ids, block_count)
    cond = one_branch(hidden_states[0], modulation[0], w_query, w_key, w_value, w_out, allowed)
    uncond = one_branch(hidden_states[1], modulation[1], w_query, w_key, w_value, w_out, allowed)
    return (uncond + guidance[0] * (cond - uncond)).astype(jnp.bfloat16)
```

```python
import functools

import jax
import jax.numpy as jnp
from jax import lax
from jax.experimental import pallas as pl
from jax.experimental.pallas import tpu as pltpu
from jax.sharding import PartitionSpec as P

HD = 64
PAIR = 2 * HD
CUTS = (2, 6, 4)
VMEM_LIMIT = 56 * 1024 * 1024


def whole(count):
    return [pl.BlockSpec(memory_space=pltpu.VMEM)] * count


def params():
    return pltpu.CompilerParams(vmem_limit_bytes=VMEM_LIMIT)


def norm_kernel(x_ref, mod_ref, h_ref):
    rows = 16
    shift = mod_ref[0:1, :]
    scale = 1.0 + mod_ref[1:2, :]

    def body(step, _):
        at = pl.ds(pl.multiple_of(step * rows, rows), rows)
        xf = x_ref[at, :].astype(jnp.float32)
        mean = jnp.mean(xf, axis=1, keepdims=True)
        cent = xf - mean
        var = jnp.mean(cent * cent, axis=1, keepdims=True)
        normed = cent / jnp.sqrt(var + 1e-05)
        h_ref[at, :] = (normed * scale + shift).astype(jnp.bfloat16)
        return 0

    lax.fori_loop(0, x_ref.shape[0] // rows, body, 0)


def norm(states, modul):
    ntok, width = states.shape
    block = 128
    return pl.pallas_call(
        norm_kernel,
        grid=(ntok // block,),
        in_specs=[
            pl.BlockSpec((block, width), lambda i: (i, 0)),
            pl.BlockSpec((3, width), lambda i: (0, 0)),
        ],
        out_specs=pl.BlockSpec((block, width), lambda i: (i, 0)),
        out_shape=jax.ShapeDtypeStruct((ntok, width), jnp.bfloat16),
        compiler_params=params(),
        cost_estimate=pl.CostEstimate(
            flops=10 * ntok * width, bytes_accessed=4 * ntok * width, transcendentals=ntok
        ),
        name="norm",
    )(states, modul)


def attend_kernel(tiles, tile_len, kmax, col, trimmed, ids_ref, own_ref, place_ref, q_ref, *refs):
    pieces, o_ref = refs[:-1], refs[-1]
    width = o_ref.shape[1]
    later = place_ref[0]

    def windows(which):
        if not trimmed:
            return which, [(0, tiles)] * len(pieces)
        last = tiles - 1
        if which == 0:
            return last * later, [(0, tiles), (0, tiles), (last * later, 1)]
        if which == last:
            return last * (1 - later), [(0, tiles), (last * (1 - later), 1), (0, tiles)]
        before, after = tiles - which, which + 1
        if before == after:
            return which, [(0, tiles), (which * (1 - later), after), (which * later, after)]
        return which, [(0, tiles)] * 3

    def row(which, slot, first, count):
        shape = (1, count * tile_len)
        lane = lax.broadcasted_iota(jnp.int32, shape, 1)
        tile = lax.div(lane, tile_len) + (own_ref[slot] + first)
        hit = tile == ids_ref[which * kmax]
        for c in range(1, kmax):
            hit = hit | (tile == ids_ref[which * kmax + c])
        return jnp.where(hit, 0.0, -1e30).astype(jnp.float32)

    lane = lax.broadcasted_iota(jnp.int32, (tile_len, PAIR), 1)
    for position in range(tiles):
        which, spans = windows(position)
        rows = pl.ds(pl.multiple_of(which * tile_len, tile_len), tile_len)
        biases = [row(which, s, f, n) for s, (f, n) in enumerate(spans)]
        keys = [pl.ds(pl.multiple_of(f * tile_len, tile_len), n * tile_len) for f, n in spans]
        for pair in range(width // PAIR):
            cols = slice(pair * PAIR, (pair + 1) * PAIR)
            vals = slice(width + pair * PAIR, width + (pair + 1) * PAIR)
            q = q_ref[rows, col + pair * PAIR : col + (pair + 1) * PAIR]
            zero = jnp.zeros_like(q)
            q2 = jnp.concatenate([jnp.where(lane < HD, q, zero), jnp.where(lane < HD, zero, q)], 0)
            scores = [
                lax.dot_general(
                    q2,
                    piece[at, cols],
                    (((1,), (1,)), ((), ())),
                    preferred_element_type=jnp.float32,
                )
                * 0.125
                + bias
                for piece, at, bias in zip(pieces, keys, biases)
            ]
            top = functools.reduce(
                jnp.maximum, [jnp.max(s, axis=1, keepdims=True) for s in scores]
            )
            expo = [jnp.exp(s - top) for s in scores]
            total = sum(jnp.sum(e, axis=1, keepdims=True) for e in expo)
            acc = sum(
                jnp.dot(e.astype(jnp.bfloat16), piece[at, vals], preferred_element_type=jnp.float32)
                for e, piece, at in zip(expo, pieces, keys)
            )
            out = acc / total
            out = jnp.where(lane < HD, out[:tile_len], out[tile_len:])
            o_ref[rows, cols] = out.astype(jnp.bfloat16)


def attend(ids, owners, place, query, pieces, col, tiles, trimmed):
    ntok = query.shape[0]
    width = pieces[0].shape[1] // 2
    kmax = ids.shape[0] // tiles
    heads = width // HD
    span = (2 * tiles + 1) * (ntok // tiles) if trimmed else len(pieces) * ntok
    smem = pl.BlockSpec(memory_space=pltpu.SMEM)
    return pl.pallas_call(
        functools.partial(attend_kernel, tiles, ntok // tiles, kmax, col, trimmed),
        in_specs=[smem] * 3 + whole(1 + len(pieces)),
        out_specs=whole(1)[0],
        out_shape=jax.ShapeDtypeStruct((ntok, width), jnp.bfloat16),
        compiler_params=params(),
        cost_estimate=pl.CostEstimate(
            flops=16 * ntok * span * heads * HD,
            bytes_accessed=4 * ntok * width * (len(pieces) + 1),
            transcendentals=ntok * span * heads,
        ),
        name="attend",
    )(ids, owners, place, query, *pieces)


def close_kernel(early_ref, own_ref, oth_ref, w_ref, c_ref, keep_a, keep_b, send_a, send_b):
    half = early_ref.shape[0] // 2
    part = early_ref.shape[1] // 4
    for p in range(4):
        cols = slice(p * part, (p + 1) * part)
        y = early_ref[:, cols]
        y += c_ref[0:1, cols] * jnp.dot(
            own_ref[...], w_ref[:, cols], preferred_element_type=jnp.float32
        )
        y += c_ref[1:2, cols] * jnp.dot(
            oth_ref[...], w_ref[:, cols], preferred_element_type=jnp.float32
        )
        a, b = y[:half], y[half:]
        at = slice((p // 2) * part, (p // 2 + 1) * part)
        if p % 2:
            send_a[:, at] = a.astype(jnp.bfloat16)
        else:
            keep_a[:, at] = a
        at = slice((p % 2) * part, (p % 2 + 1) * part)
        if p // 2:
            send_b[:, at] = b.astype(jnp.bfloat16)
        else:
            keep_b[:, at] = b


def close(early, own, oth, w_last, coef):
    ntok, width = early.shape
    keep = jax.ShapeDtypeStruct((ntok // 2, width // 2), jnp.float32)
    send = jax.ShapeDtypeStruct((ntok // 2, width // 2), jnp.bfloat16)
    return pl.pallas_call(
        close_kernel,
        in_specs=whole(5),
        out_specs=whole(4),
        out_shape=[keep, keep, send, send],
        compiler_params=params(),
        cost_estimate=pl.CostEstimate(
            flops=4 * ntok * width * own.shape[1], bytes_accessed=8 * ntok * width, transcendentals=0
        ),
        name="close",
    )(early, own, oth, w_last, coef)


def neighbours(value, distance):
    count = lax.axis_size("seq")
    firsts = [i for i in range(count - distance) if (i // distance) % 2 == 0]
    seconds = [i for i in range(count - distance) if (i // distance) % 2 == 1]
    out = []
    for lows in (firsts, seconds):
        route = [(i, i + distance) for i in lows] + [(i + distance, i) for i in lows]
        out.append(lax.ppermute(value, "seq", route))
    return out


def crossed(value, axis, bit):
    return lax.ppermute(value, axis, [(i, i ^ bit) for i in range(lax.axis_size(axis))])


def shards(
    hidden_states, modulation, w_query, w_key, w_value, w_out, block_ids, block_count, guidance
):
    states = hidden_states[0]
    modul = modulation[0]
    ntok, model = states.shape
    tiles, kmax = block_ids.shape
    heads = w_query.shape[1] // HD
    branch = lax.axis_index("guid")
    tp_here = lax.axis_index("tp")
    seq_here = lax.axis_index("seq")
    seq_count = lax.axis_size("seq")
    reach_dev = min(4, (seq_count - 1) // 2)
    part = model // (2 * lax.axis_size("tp"))
    cuts = [c * heads // sum(CUTS) for c in CUTS]
    starts = [sum(cuts[:i]) for i in range(len(cuts))]

    live = jnp.arange(kmax, dtype=jnp.int32)[None, :] < block_count[:, None]
    ids = jnp.where(live, block_ids, -(1 << 20)).reshape(-1)
    owners = [seq_here]
    for distance in range(1, reach_dev + 1):
        ahead = (seq_here // distance) % 2 == 0
        owners += [
            jnp.where(ahead, seq_here + distance, seq_here - distance),
            jnp.where(ahead, seq_here - distance, seq_here + distance),
        ]
    place = (seq_here % 2 == 0).astype(jnp.int32).reshape(1)
    owners = jnp.stack(owners).astype(jnp.int32) * tiles

    h = norm(states, modul)

    def project(weight):
        return jnp.dot(h, weight, preferred_element_type=jnp.float32).astype(jnp.bfloat16)

    slots = []
    for first, count in zip(starts, cuts):
        cols = slice(first * HD, (first + count) * HD)
        piece = jnp.concatenate([project(w_key[:, cols]), project(w_value[:, cols])], axis=1)
        near = [piece]
        for distance in range(1, reach_dev + 1):
            near += neighbours(piece, distance)
        slots.append(near)
    query = project(w_query)

    scale = guidance[0]
    mine = jnp.where(branch == 0, scale, 1.0 - scale)
    others = jnp.where(branch == 0, 1.0 - scale, scale)
    here = branch * (model // 2)
    there = (1 - branch) * (model // 2)
    x_there = lax.dynamic_slice(states, (0, there + tp_here * part), (ntok, part))
    x_here = lax.dynamic_slice(states, (0, here + tp_here * part), (ntok, part))
    x_other = crossed(x_there, "guid", 1)
    gate_other = crossed(lax.dynamic_slice(modul, (2, there), (1, model // 2)), "guid", 1)
    gate_own = lax.dynamic_slice(modul, (2, here), (1, model // 2))
    coef = jnp.concatenate([mine * gate_own, others * gate_other], axis=0)
    base = mine * x_here.astype(jnp.float32) + others * x_other.astype(jnp.float32)

    def by_partner(array, offset):
        return jnp.concatenate(
            [
                lax.dynamic_slice(
                    array, (0, offset + (tp_here ^ p) * part), (array.shape[0], part)
                )
                for p in range(4)
            ],
            axis=1,
        )

    w_here = by_partner(w_out, here)
    coef = by_partner(coef, 0)

    own, other = [], []
    for first, near in zip(starts, slots):
        out = attend(ids, owners, place, query, near, first * HD, tiles, reach_dev == 1)
        own.append(out)
        other.append(crossed(out, "guid", 1))

    last = starts[-1] * HD
    early = coef[0:1] * jnp.dot(
        jnp.concatenate(own[:-1], axis=1), w_here[:last], preferred_element_type=jnp.float32
    ) + coef[1:2] * jnp.dot(
        jnp.concatenate(other[:-1], axis=1), w_here[:last], preferred_element_type=jnp.float32
    )
    keep_a, keep_b, send_a, send_b = close(early, own[-1], other[-1], w_here[last:], coef)
    got_a = crossed(send_a, "tp", 1)
    got_b = crossed(send_b, "tp", 2)
    sum_a = keep_a + got_a.astype(jnp.float32)
    sum_b = keep_b + got_b.astype(jnp.float32)
    last_a = crossed(sum_a[:, part:].astype(jnp.bfloat16), "tp", 2)
    last_b = crossed(sum_b[:, part:].astype(jnp.bfloat16), "tp", 1)
    total = jnp.concatenate(
        [
            sum_a[:, :part] + last_a.astype(jnp.float32),
            sum_b[:, :part] + last_b.astype(jnp.float32),
        ],
        axis=0,
    )
    return (base + total).astype(jnp.bfloat16)


def solution(mesh):
    in_specs = (
        P("guid", "seq", None),
        P("guid", None, None),
        P(None, "tp"),
        P(None, "tp"),
        P(None, "tp"),
        P("tp", None),
        P("seq", None),
        P("seq"),
        P(),
    )
    out_specs = P("seq", ("guid", "tp"))
    return jax.shard_map(shards, mesh=mesh, in_specs=in_specs, out_specs=out_specs, check_vma=False)
```

```python
import functools

import jax
import jax.numpy as jnp
from jax import lax
from jax.experimental import pallas as pl
from jax.experimental.pallas import tpu as pltpu
from jax.sharding import PartitionSpec as P

HD = 64
PAIR = 2 * HD
FIRST_VALUES = 8 / 12
MIB = 1024 * 1024


def vmem(count):
    return [pl.BlockSpec(memory_space=pltpu.VMEM)] * count


def smem(count):
    return [pl.BlockSpec(memory_space=pltpu.SMEM)] * count


def params(mib):
    return pltpu.CompilerParams(vmem_limit_bytes=mib * MIB)


def cost(flops, nbytes, exps=0):
    return pl.CostEstimate(flops=int(flops), bytes_accessed=int(nbytes), transcendentals=int(exps))


def aligned(start, size):
    return pl.ds(pl.multiple_of(start, 128), size)


def norm_kernel(x_ref, mod_ref, h_ref):
    rows = 64
    shift = mod_ref[0]
    scale = 1.0 + mod_ref[1]
    for step in range(h_ref.shape[0] // rows):
        at = slice(step * rows, (step + 1) * rows)
        xf = x_ref[0, at, :].astype(jnp.float32)
        cent = xf - jnp.mean(xf, axis=1, keepdims=True)
        var = jnp.mean(cent * cent, axis=1, keepdims=True)
        h_ref[at, :] = (cent / jnp.sqrt(var + 1e-05) * scale + shift).astype(jnp.bfloat16)


def norm(states, modul):
    _, ntok, width = states.shape
    block = 128
    return pl.pallas_call(
        norm_kernel,
        grid=(ntok // block,),
        in_specs=[
            pl.BlockSpec((1, block, width), lambda i: (0, i, 0)),
            pl.BlockSpec((3, 1, width), lambda i: (0, 0, 0)),
        ],
        out_specs=pl.BlockSpec((block, width), lambda i: (i, 0)),
        out_shape=jax.ShapeDtypeStruct((ntok, width), jnp.bfloat16),
        compiler_params=params(12),
        cost_estimate=cost(10 * ntok * width, 4 * ntok * width, ntok),
        name="norm",
    )(states, modul)


def ahead_here(distance):
    return 1 - lax.rem(lax.div(lax.axis_index("seq"), distance), 2)


def spans_of(position, tiles, slots, trimmed):
    if not trimmed:
        return position, [(0, tiles)] * slots
    ahead, last = ahead_here(1), tiles - 1
    if position == 0:
        return last * ahead, [(0, tiles), (0, tiles), (last * ahead, 1)]
    if position == last:
        return last * (1 - ahead), [(0, tiles), (last * (1 - ahead), 1), (0, tiles)]
    if tiles - position == position + 1:
        count = position + 1
        return position, [(0, tiles), (position * (1 - ahead), count), (position * ahead, count)]
    return position, [(0, tiles)] * 3


def bias_rows(which, spans, tile_len, ids_ref, count_ref):
    here, tiles = lax.axis_index("seq"), ids_ref.shape[0]
    owners = [here]
    for distance in range(1, (len(spans) - 1) // 2 + 1):
        side = 2 * ahead_here(distance) - 1
        owners += [here + side * distance, here - side * distance]
    kmax = ids_ref.shape[1]
    live = count_ref[which]
    listed = [jnp.where(c < live, ids_ref[which, c], ids_ref[which, 0]) for c in range(kmax)]
    out = []
    for owner, (first, count) in zip(owners, spans):
        lane = lax.broadcasted_iota(jnp.int32, (1, count * tile_len), 1)
        tile = lax.div(lane, tile_len) + (owner * tiles + first)
        hit = functools.reduce(jnp.logical_or, [tile == one for one in listed])
        out.append(jnp.where(hit, 0.0, -1e30).astype(jnp.float32))
    return out


def score(q, keys, biases):
    lane = lax.broadcasted_iota(jnp.int32, q.shape, 1)
    q = q * jnp.asarray(0.125, q.dtype)
    zero = jnp.zeros_like(q)
    both = jnp.concatenate([jnp.where(lane < HD, q, zero), jnp.where(lane < HD, zero, q)], 0)
    return [
        lax.dot_general(both, k, (((1,), (1,)), ((), ())), preferred_element_type=jnp.float32) + b
        for k, b in zip(keys, biases)
    ]


def soften(scores):
    top = functools.reduce(jnp.maximum, [jnp.max(s, axis=1, keepdims=True) for s in scores])
    expo = [jnp.exp(s - top) for s in scores]
    total = sum(jnp.sum(e, axis=1, keepdims=True) for e in expo)
    return [e.astype(jnp.bfloat16) for e in expo], 1.0 / total


def by_head(stacked, width):
    half = stacked.shape[0] // 2
    lane = lax.broadcasted_iota(jnp.int32, (half, width), 1)
    return jnp.where(lane < HD, stacked[:half], stacked[half:])


def plan(tiles, tile_len, slots, trimmed, pairs):
    items = []
    for position in range(tiles):
        which, spans = spans_of(position, tiles, slots, trimmed)
        rows = pl.ds(pl.multiple_of(which * tile_len, tile_len), tile_len)
        keys = [pl.ds(pl.multiple_of(f * tile_len, tile_len), n * tile_len) for f, n in spans]
        items += [(position, which, spans, rows, keys, pair) for pair in range(pairs)]
    return items


def overlapped(items, begin, end):
    current = begin(items[0])
    for i, item in enumerate(items):
        following = begin(items[i + 1]) if i + 1 < len(items) else None
        end(item, current)
        current = following


def columns(pair):
    return slice(pair * PAIR, (pair + 1) * PAIR)


def weigh_kernel(tiles, trimmed, ids_ref, count_ref, q_ref, *refs):
    pieces, p_ref, inv_ref = refs[:-2], refs[-2], refs[-1]
    tile_len = q_ref.shape[0] // tiles
    pairs = q_ref.shape[1] // PAIR
    rows_of = {}

    def begin(item):
        position, which, spans, rows, keys, pair = item
        if position not in rows_of:
            rows_of[position] = bias_rows(which, spans, tile_len, ids_ref, count_ref)
        near = [piece[at, columns(pair)] for piece, at in zip(pieces, keys)]
        return score(q_ref[rows, columns(pair)], near, rows_of[position])

    def end(item, scores):
        position, which, spans, rows, keys, pair = item
        expo, inverse = soften(scores)
        slot, at = position * pairs + pair, 0
        for e in expo:
            p_ref[slot, :, at : at + e.shape[1]] = e
            at += e.shape[1]
        inv_ref[slot] = by_head(inverse, PAIR)

    overlapped(plan(tiles, tile_len, len(pieces), trimmed, pairs), begin, end)


def weigh(block_ids, block_count, query, pieces, span):
    ntok, width = query.shape
    tiles = block_ids.shape[0]
    items = tiles * width // PAIR
    tile_len = ntok // tiles
    return pl.pallas_call(
        functools.partial(weigh_kernel, tiles, True),
        in_specs=smem(2) + vmem(1 + len(pieces)),
        out_specs=vmem(2),
        out_shape=[
            jax.ShapeDtypeStruct((items, 2 * tile_len, span), jnp.bfloat16),
            jax.ShapeDtypeStruct((items, tile_len, PAIR), jnp.float32),
        ],
        compiler_params=params(24),
        cost_estimate=cost(4 * ntok * span * width, 2 * ntok * span * width / HD, ntok * span * width / HD),
        name="weigh",
    )(block_ids, block_count, query, *pieces)


def gather_kernel(tiles, first_pair, p_ref, inv_ref, *refs):
    pieces, o_ref = refs[:-1], refs[-1]
    tile_len = o_ref.shape[0] // tiles
    pairs = o_ref.shape[1] // PAIR
    all_pairs = p_ref.shape[0] // tiles
    for position, which, spans, rows, keys, pair in plan(tiles, tile_len, len(pieces), True, pairs):
        slot, start, acc = position * all_pairs + first_pair + pair, 0, 0.0
        for piece, at, (_, count) in zip(pieces, keys, spans):
            part = p_ref[slot, :, start : start + count * tile_len]
            acc += jnp.dot(part, piece[at, columns(pair)], preferred_element_type=jnp.float32)
            start += count * tile_len
        o_ref[rows, columns(pair)] = (by_head(acc, PAIR) * inv_ref[slot]).astype(jnp.bfloat16)


def gather(p, inv, pieces, first_pair, tiles):
    ntok, width = pieces[0].shape
    return pl.pallas_call(
        functools.partial(gather_kernel, tiles, first_pair),
        in_specs=vmem(2 + len(pieces)),
        out_specs=vmem(1)[0],
        out_shape=jax.ShapeDtypeStruct((ntok, width), jnp.bfloat16),
        compiler_params=params(24),
        cost_estimate=cost(4 * ntok * p.shape[2] * width, 2 * ntok * p.shape[2] * width / HD),
        name="gather",
    )(p, inv, *pieces)


def attend_kernel(tiles, slots, ids_ref, count_ref, q_ref, *refs):
    keys_refs, values, o_ref = refs[:slots], refs[slots : 2 * slots], refs[-1]
    tile_len = q_ref.shape[0] // tiles
    for position, which, spans, rows, keys, pair in plan(
        tiles, tile_len, slots, False, o_ref.shape[1] // PAIR
    ):
        biases = bias_rows(which, spans, tile_len, ids_ref, count_ref)
        near = [piece[at, columns(pair)] for piece, at in zip(keys_refs, keys)]
        expo, inverse = soften(score(q_ref[rows, columns(pair)], near, biases))
        acc = sum(
            jnp.dot(e, piece[at, columns(pair)], preferred_element_type=jnp.float32)
            for e, piece, at in zip(expo, values, keys)
        )
        o_ref[rows, columns(pair)] = by_head(acc * inverse, PAIR).astype(jnp.bfloat16)


def attend(block_ids, block_count, query, keys, values):
    ntok, width = query.shape
    span = ntok * len(keys)
    return pl.pallas_call(
        functools.partial(attend_kernel, block_ids.shape[0], len(keys)),
        in_specs=smem(2) + vmem(1 + 2 * len(keys)),
        out_specs=vmem(1)[0],
        out_shape=jax.ShapeDtypeStruct((ntok, width), jnp.bfloat16),
        compiler_params=params(40),
        cost_estimate=cost(8 * ntok * span * width, 4 * span * width, ntok * span * width / HD),
        name="attend",
    )(block_ids, block_count, query, *keys, *values)


def early_kernel(own_ref, oth_ref, w_hbm, x_hbm, xo_ref, mod_ref, gate_ref, scale_ref, *refs):
    y_ref, wl_ref, c_ref, wb, xb, sems = refs
    part = xb.shape[1]
    model = x_hbm.shape[2]
    done = own_ref.shape[1]
    branch, here = lax.axis_index("guid"), lax.axis_index("tp")
    starts = [branch * (model // 2) + lax.bitwise_xor(here, p) * part for p in range(4)]
    spots = [slice(p * part, (p + 1) * part) for p in range(4)]
    copies = [
        pltpu.make_async_copy(x_hbm.at[0, :, aligned(starts[0], part)], xb, sems.at[8])
    ]
    for p in range(4):
        src = w_hbm.at[pl.ds(0, done), aligned(starts[p], part)]
        copies.append(pltpu.make_async_copy(src, wb.at[:, spots[p]], sems.at[p]))
    for p in range(4):
        src = w_hbm.at[pl.ds(done, wl_ref.shape[0]), aligned(starts[p], part)]
        copies.append(pltpu.make_async_copy(src, wl_ref.at[:, spots[p]], sems.at[4 + p]))
    for copy in copies:
        copy.start()
    scale = scale_ref[0]
    mine = jnp.where(branch == 0, scale, 1.0 - scale)
    others = jnp.where(branch == 0, 1.0 - scale, scale)
    copies[0].wait()
    base = mine * xb[...].astype(jnp.float32) + others * xo_ref[...].astype(jnp.float32)
    for p in range(4):
        at = aligned(starts[p], part)
        own_gate = mine * mod_ref[2, :, at]
        oth_gate = others * gate_ref[0, :, at]
        c_ref[0:1, spots[p]] = own_gate
        c_ref[1:2, spots[p]] = oth_gate
        copies[1 + p].wait()
        weight = wb[:, spots[p]]
        y = own_gate * jnp.dot(own_ref[...], weight, preferred_element_type=jnp.float32)
        y += oth_gate * jnp.dot(oth_ref[...], weight, preferred_element_type=jnp.float32)
        y_ref[:, spots[p]] = y + base if p == 0 else y
    for copy in copies[5:]:
        copy.wait()


def early(own, oth, w_out, states, x_other, modul, gate_other, scale):
    ntok, done = own.shape
    width, model = w_out.shape
    part = x_other.shape[1]
    hbm = [pl.BlockSpec(memory_space=pl.ANY)]
    return pl.pallas_call(
        early_kernel,
        in_specs=vmem(2) + hbm * 2 + vmem(3) + smem(1),
        out_specs=vmem(3),
        out_shape=[
            jax.ShapeDtypeStruct((ntok, model // 2), jnp.float32),
            jax.ShapeDtypeStruct((width - done, model // 2), jnp.bfloat16),
            jax.ShapeDtypeStruct((2, model // 2), jnp.float32),
        ],
        scratch_shapes=[
            pltpu.VMEM((done, model // 2), jnp.bfloat16),
            pltpu.VMEM((ntok, part), jnp.bfloat16),
            pltpu.SemaphoreType.DMA((9,)),
        ],
        compiler_params=params(16),
        cost_estimate=cost(2 * ntok * model * done, width * model + 4 * ntok * model),
        name="early",
    )(own, oth, w_out, states, x_other, modul, gate_other, scale)


def close_kernel(early_ref, own_ref, oth_ref, w_ref, c_ref, keep_a, keep_b, send_a, send_b):
    half = early_ref.shape[0] // 2
    part = early_ref.shape[1] // 4
    for p in (3, 1, 2, 0):
        cols = slice(p * part, (p + 1) * part)
        y = early_ref[:, cols]
        y += c_ref[0:1, cols] * jnp.dot(
            own_ref[...], w_ref[:, cols], preferred_element_type=jnp.float32
        )
        y += c_ref[1:2, cols] * jnp.dot(
            oth_ref[...], w_ref[:, cols], preferred_element_type=jnp.float32
        )
        a, b = y[:half], y[half:]
        at = slice((p // 2) * part, (p // 2 + 1) * part)
        if p % 2:
            send_a[:, at] = a.astype(jnp.bfloat16)
        else:
            keep_a[:, at] = a
        at = slice((p % 2) * part, (p % 2 + 1) * part)
        if p // 2:
            send_b[:, at] = b.astype(jnp.bfloat16)
        else:
            keep_b[:, at] = b


def close(sofar, own, oth, w_last, coef):
    ntok, width = sofar.shape
    keep = jax.ShapeDtypeStruct((ntok // 2, width // 2), jnp.float32)
    send = jax.ShapeDtypeStruct((ntok // 2, width // 2), jnp.bfloat16)
    return pl.pallas_call(
        close_kernel,
        in_specs=vmem(5),
        out_specs=vmem(4),
        out_shape=[keep, keep, send, send],
        compiler_params=params(16),
        cost_estimate=cost(4 * ntok * width * own.shape[1], 8 * ntok * width),
        name="close",
    )(sofar, own, oth, w_last, coef)


def neighbours(value, distance):
    count = lax.axis_size("seq")
    out = []
    for odd in (0, 1):
        lows = [i for i in range(count - distance) if (i // distance) % 2 == odd]
        route = [(i, i + distance) for i in lows] + [(i + distance, i) for i in lows]
        out.append(lax.ppermute(value, "seq", route))
    return out


def crossed(value, axis, bit):
    return lax.ppermute(value, axis, [(i, i ^ bit) for i in range(lax.axis_size(axis))])


def shards(
    hidden_states, modulation, w_query, w_key, w_value, w_out, block_ids, block_count, guidance
):
    _, ntok, model = hidden_states.shape
    tiles = block_ids.shape[0]
    width = w_query.shape[1]
    branch = lax.axis_index("guid")
    tp_here = lax.axis_index("tp")
    reach_dev = min(4, (lax.axis_size("seq") - 1) // 2)
    part = model // (2 * lax.axis_size("tp"))
    cut = int(width * FIRST_VALUES) // PAIR * PAIR
    modul = jnp.transpose(modulation, (1, 0, 2))

    h = norm(hidden_states, modul)

    def project(weight):
        return jnp.dot(h, weight, preferred_element_type=jnp.float32).astype(jnp.bfloat16)

    def near(value):
        out = [value]
        for distance in range(1, reach_dev + 1):
            out += neighbours(value, distance)
        return out

    keys = near(project(w_key))
    value = project(w_value)
    values = [near(value[:, :cut]), near(value[:, cut:])]
    query = project(w_query)

    there = (1 - branch) * (model // 2) + tp_here * part
    x_other = crossed(lax.dynamic_slice_in_dim(hidden_states[0], there, part, 1), "guid", 1)
    gate_other = crossed(modul[2:3], "guid", 1)

    if reach_dev == 1:
        span = (2 * tiles + 1) * (ntok // tiles)
        p, inv = weigh(block_ids, block_count, query, keys, span)
        own = [gather(p, inv, values[0], 0, tiles), gather(p, inv, values[1], cut // PAIR, tiles)]
    else:
        own = [
            attend(block_ids, block_count, query[:, at], [k[:, at] for k in keys], v)
            for at, v in zip((slice(0, cut), slice(cut, width)), values)
        ]
    other = [crossed(one, "guid", 1) for one in own]

    sofar, w_last, coef = early(
        own[0], other[0], w_out, hidden_states, x_other, modul, gate_other, guidance
    )
    keep_a, keep_b, send_a, send_b = close(sofar, own[1], other[1], w_last, coef)
    got_a = crossed(send_a, "tp", 1)
    got_b = crossed(send_b, "tp", 2)
    sum_a = keep_a + got_a.astype(jnp.float32)
    sum_b = keep_b + got_b.astype(jnp.float32)
    last_a = crossed(sum_a[:, part:].astype(jnp.bfloat16), "tp", 2)
    last_b = crossed(sum_b[:, part:].astype(jnp.bfloat16), "tp", 1)
    return jnp.concatenate(
        [
            (sum_a[:, :part] + last_a.astype(jnp.float32)).astype(jnp.bfloat16),
            (sum_b[:, :part] + last_b.astype(jnp.float32)).astype(jnp.bfloat16),
        ],
        axis=0,
    )


def solution(mesh):
    in_specs = (
        P("guid", "seq", None),
        P("guid", None, None),
        P(None, "tp"),
        P(None, "tp"),
        P(None, "tp"),
        P("tp", None),
        P("seq", None),
        P("seq"),
        P(),
    )
    out_specs = P("seq", ("guid", "tp"))
    return jax.shard_map(shards, mesh=mesh, in_specs=in_specs, out_specs=out_specs, check_vma=False)
```

```python
import functools

import jax
import jax.numpy as jnp
from jax import lax
from jax.experimental import pallas as pl
from jax.experimental.pallas import tpu as pltpu
from jax.sharding import PartitionSpec as P

HD = 64
PAIR = 2 * HD
FIRST_VALUES = 8 / 12
MIB = 1024 * 1024


def vmem(count):
    return [pl.BlockSpec(memory_space=pltpu.VMEM)] * count


def smem(count):
    return [pl.BlockSpec(memory_space=pltpu.SMEM)] * count


def params(mib):
    return pltpu.CompilerParams(vmem_limit_bytes=mib * MIB)


def cost(flops, nbytes, exps=0):
    return pl.CostEstimate(flops=int(flops), bytes_accessed=int(nbytes), transcendentals=int(exps))


def aligned(start, size):
    return pl.ds(pl.multiple_of(start, 128), size)


def norm_kernel(x_ref, mod_ref, h_ref):
    rows = 64
    shift = mod_ref[0]
    scale = 1.0 + mod_ref[1]
    for step in range(h_ref.shape[0] // rows):
        at = slice(step * rows, (step + 1) * rows)
        xf = x_ref[0, at, :].astype(jnp.float32)
        cent = xf - jnp.mean(xf, axis=1, keepdims=True)
        var = jnp.mean(cent * cent, axis=1, keepdims=True)
        h_ref[at, :] = (cent / jnp.sqrt(var + 1e-05) * scale + shift).astype(jnp.bfloat16)


def norm(states, modul):
    _, ntok, width = states.shape
    block = 128
    return pl.pallas_call(
        norm_kernel,
        grid=(ntok // block,),
        in_specs=[
            pl.BlockSpec((1, block, width), lambda i: (0, i, 0)),
            pl.BlockSpec((3, 1, width), lambda i: (0, 0, 0)),
        ],
        out_specs=pl.BlockSpec((block, width), lambda i: (i, 0)),
        out_shape=jax.ShapeDtypeStruct((ntok, width), jnp.bfloat16),
        compiler_params=params(12),
        cost_estimate=cost(10 * ntok * width, 4 * ntok * width, ntok),
        name="norm",
    )(states, modul)


def ahead_here(distance):
    return 1 - lax.rem(lax.div(lax.axis_index("seq"), distance), 2)


def spans_of(position, tiles, slots, trimmed):
    if not trimmed:
        return position, [(0, tiles)] * slots
    ahead, last = ahead_here(1), tiles - 1
    if position == 0:
        return last * ahead, [(0, tiles), (0, tiles), (last * ahead, 1)]
    if position == last:
        return last * (1 - ahead), [(0, tiles), (last * (1 - ahead), 1), (0, tiles)]
    if tiles - position == position + 1:
        count = position + 1
        return position, [(0, tiles), (position * (1 - ahead), count), (position * ahead, count)]
    return position, [(0, tiles)] * 3


def bias_rows(which, spans, tile_len, ids_ref, count_ref):
    here, tiles = lax.axis_index("seq"), ids_ref.shape[0]
    owners = [here]
    for distance in range(1, (len(spans) - 1) // 2 + 1):
        side = 2 * ahead_here(distance) - 1
        owners += [here + side * distance, here - side * distance]
    kmax = ids_ref.shape[1]
    live = count_ref[which]
    listed = [jnp.where(c < live, ids_ref[which, c], ids_ref[which, 0]) for c in range(kmax)]
    out = []
    for owner, (first, count) in zip(owners, spans):
        lane = lax.broadcasted_iota(jnp.int32, (1, count * tile_len), 1)
        tile = lax.div(lane, tile_len) + (owner * tiles + first)
        hit = functools.reduce(jnp.logical_or, [tile == one for one in listed])
        out.append(jnp.where(hit, 0.0, -1e30).astype(jnp.float32))
    return out


def score(q, keys, biases):
    lane = lax.broadcasted_iota(jnp.int32, q.shape, 1)
    q = q * jnp.asarray(0.125, q.dtype)
    zero = jnp.zeros_like(q)
    both = jnp.concatenate([jnp.where(lane < HD, q, zero), jnp.where(lane < HD, zero, q)], 0)
    return [
        lax.dot_general(both, k, (((1,), (1,)), ((), ())), preferred_element_type=jnp.float32) + b
        for k, b in zip(keys, biases)
    ]


def soften(scores):
    top = functools.reduce(jnp.maximum, [jnp.max(s, axis=1, keepdims=True) for s in scores])
    expo = [jnp.exp(s - top) for s in scores]
    total = sum(jnp.sum(e, axis=1, keepdims=True) for e in expo)
    return [e.astype(jnp.bfloat16) for e in expo], 1.0 / total


def by_head(stacked, width):
    half = stacked.shape[0] // 2
    lane = lax.broadcasted_iota(jnp.int32, (half, width), 1)
    return jnp.where(lane < HD, stacked[:half], stacked[half:])


def plan(tiles, tile_len, slots, trimmed, pairs):
    items = []
    for position in range(tiles):
        which, spans = spans_of(position, tiles, slots, trimmed)
        rows = pl.ds(pl.multiple_of(which * tile_len, tile_len), tile_len)
        keys = [pl.ds(pl.multiple_of(f * tile_len, tile_len), n * tile_len) for f, n in spans]
        items += [(position, which, spans, rows, keys, pair) for pair in range(pairs)]
    return items


def overlapped(items, begin, end):
    current = begin(items[0])
    for i, item in enumerate(items):
        following = begin(items[i + 1]) if i + 1 < len(items) else None
        end(item, current)
        current = following


def columns(pair):
    return slice(pair * PAIR, (pair + 1) * PAIR)


def weigh_kernel(tiles, trimmed, ids_ref, count_ref, q_ref, *refs):
    pieces, p_ref, inv_ref = refs[:-2], refs[-2], refs[-1]
    tile_len = q_ref.shape[0] // tiles
    pairs = q_ref.shape[1] // PAIR
    rows_of = {}

    def begin(item):
        position, which, spans, rows, keys, pair = item
        if position not in rows_of:
            rows_of[position] = bias_rows(which, spans, tile_len, ids_ref, count_ref)
        near = [piece[at, columns(pair)] for piece, at in zip(pieces, keys)]
        return score(q_ref[rows, columns(pair)], near, rows_of[position])

    def end(item, scores):
        position, which, spans, rows, keys, pair = item
        expo, inverse = soften(scores)
        slot, at = position * pairs + pair, 0
        for e in expo:
            p_ref[slot, :, at : at + e.shape[1]] = e
            at += e.shape[1]
        inv_ref[slot] = by_head(inverse, PAIR)

    overlapped(plan(tiles, tile_len, len(pieces), trimmed, pairs), begin, end)


def weigh(block_ids, block_count, query, pieces, span):
    ntok, width = query.shape
    tiles = block_ids.shape[0]
    items = tiles * width // PAIR
    tile_len = ntok // tiles
    return pl.pallas_call(
        functools.partial(weigh_kernel, tiles, True),
        in_specs=smem(2) + vmem(1 + len(pieces)),
        out_specs=vmem(2),
        out_shape=[
            jax.ShapeDtypeStruct((items, 2 * tile_len, span), jnp.bfloat16),
            jax.ShapeDtypeStruct((items, tile_len, PAIR), jnp.float32),
        ],
        compiler_params=params(24),
        cost_estimate=cost(4 * ntok * span * width, 2 * ntok * span * width / HD, ntok * span * width / HD),
        name="weigh",
    )(block_ids, block_count, query, *pieces)


def gather_kernel(tiles, first_pair, p_ref, inv_ref, _, *refs):
    pieces, o_ref = refs[:-1], refs[-1]
    tile_len = o_ref.shape[0] // tiles
    pairs = o_ref.shape[1] // PAIR
    all_pairs = p_ref.shape[0] // tiles
    for position, which, spans, rows, keys, pair in plan(tiles, tile_len, len(pieces), True, pairs):
        slot, start, acc = position * all_pairs + first_pair + pair, 0, 0.0
        for piece, at, (_, count) in zip(pieces, keys, spans):
            part = p_ref[slot, :, start : start + count * tile_len]
            acc += jnp.dot(part, piece[at, columns(pair)], preferred_element_type=jnp.float32)
            start += count * tile_len
        o_ref[rows, columns(pair)] = (by_head(acc, PAIR) * inv_ref[slot]).astype(jnp.bfloat16)


def gather(p, inv, after, pieces, first_pair, tiles):
    ntok, width = pieces[0].shape
    return pl.pallas_call(
        functools.partial(gather_kernel, tiles, first_pair),
        in_specs=vmem(2) + [pl.BlockSpec(memory_space=pl.ANY)] + vmem(len(pieces)),
        out_specs=vmem(1)[0],
        out_shape=jax.ShapeDtypeStruct((ntok, width), jnp.bfloat16),
        compiler_params=params(24),
        cost_estimate=cost(2e10, 2 * ntok * p.shape[2] * width / HD),
        name="gather",
    )(p, inv, after, *pieces)


def attend_kernel(tiles, slots, ids_ref, count_ref, q_ref, *refs):
    keys_refs, values, o_ref = refs[:slots], refs[slots : 2 * slots], refs[-1]
    tile_len = q_ref.shape[0] // tiles
    for position, which, spans, rows, keys, pair in plan(
        tiles, tile_len, slots, False, o_ref.shape[1] // PAIR
    ):
        biases = bias_rows(which, spans, tile_len, ids_ref, count_ref)
        near = [piece[at, columns(pair)] for piece, at in zip(keys_refs, keys)]
        expo, inverse = soften(score(q_ref[rows, columns(pair)], near, biases))
        acc = sum(
            jnp.dot(e, piece[at, columns(pair)], preferred_element_type=jnp.float32)
            for e, piece, at in zip(expo, values, keys)
        )
        o_ref[rows, columns(pair)] = by_head(acc * inverse, PAIR).astype(jnp.bfloat16)


def attend(block_ids, block_count, query, keys, values):
    ntok, width = query.shape
    span = ntok * len(keys)
    return pl.pallas_call(
        functools.partial(attend_kernel, block_ids.shape[0], len(keys)),
        in_specs=smem(2) + vmem(1 + 2 * len(keys)),
        out_specs=vmem(1)[0],
        out_shape=jax.ShapeDtypeStruct((ntok, width), jnp.bfloat16),
        compiler_params=params(40),
        cost_estimate=cost(8 * ntok * span * width, 4 * span * width, ntok * span * width / HD),
        name="attend",
    )(block_ids, block_count, query, *keys, *values)


def partner_starts(model, part):
    branch, here = lax.axis_index("guid"), lax.axis_index("tp")
    return [branch * (model // 2) + lax.bitwise_xor(here, p) * part for p in range(4)]


def early_kernel(own_ref, oth_ref, w_ref, x_hbm, xo_ref, mod_ref, gate_ref, scale_ref, *refs):
    y_ref, c_ref, xb, sem = refs
    part = xb.shape[1]
    done = own_ref.shape[1]
    starts = partner_starts(x_hbm.shape[2], part)
    copy = pltpu.make_async_copy(x_hbm.at[0, :, aligned(starts[0], part)], xb, sem)
    copy.start()
    scale = scale_ref[0]
    branch = lax.axis_index("guid")
    mine = jnp.where(branch == 0, scale, 1.0 - scale)
    others = jnp.where(branch == 0, 1.0 - scale, scale)
    for p in (3, 2, 1, 0):
        at = aligned(starts[p], part)
        spot = slice(p * part, (p + 1) * part)
        own_gate = mine * mod_ref[2, :, at]
        oth_gate = others * gate_ref[0, :, at]
        c_ref[0:1, spot] = own_gate
        c_ref[1:2, spot] = oth_gate
        weight = w_ref[0:done, at]
        y = own_gate * jnp.dot(own_ref[...], weight, preferred_element_type=jnp.float32)
        y += oth_gate * jnp.dot(oth_ref[...], weight, preferred_element_type=jnp.float32)
        if p == 0:
            copy.wait()
            y += mine * xb[...].astype(jnp.float32) + others * xo_ref[...].astype(jnp.float32)
        y_ref[:, spot] = y


def early(own, oth, w_out, states, x_other, modul, gate_other, scale):
    ntok, done = own.shape
    width, model = w_out.shape
    part = x_other.shape[1]
    return pl.pallas_call(
        early_kernel,
        in_specs=vmem(3) + [pl.BlockSpec(memory_space=pl.ANY)] + vmem(3) + smem(1),
        out_specs=vmem(2),
        out_shape=[
            jax.ShapeDtypeStruct((ntok, model // 2), jnp.float32),
            jax.ShapeDtypeStruct((2, model // 2), jnp.float32),
        ],
        scratch_shapes=[pltpu.VMEM((ntok, part), jnp.bfloat16), pltpu.SemaphoreType.DMA],
        compiler_params=params(16),
        cost_estimate=cost(2 * ntok * model * done, width * model + 4 * ntok * model),
        name="early",
    )(own, oth, w_out, states, x_other, modul, gate_other, scale)


def close_kernel(early_ref, own_ref, oth_ref, w_ref, c_ref, keep_a, keep_b, send_a, send_b):
    half = early_ref.shape[0] // 2
    part = early_ref.shape[1] // 4
    first = w_ref.shape[0] - own_ref.shape[1]
    starts = partner_starts(w_ref.shape[1], part)
    for p in (3, 1, 2, 0):
        cols = slice(p * part, (p + 1) * part)
        weight = w_ref[first:, aligned(starts[p], part)]
        y = early_ref[:, cols]
        y += c_ref[0:1, cols] * jnp.dot(own_ref[...], weight, preferred_element_type=jnp.float32)
        y += c_ref[1:2, cols] * jnp.dot(oth_ref[...], weight, preferred_element_type=jnp.float32)
        a, b = y[:half], y[half:]
        at = slice((p // 2) * part, (p // 2 + 1) * part)
        if p % 2:
            send_a[:, at] = a.astype(jnp.bfloat16)
        else:
            keep_a[:, at] = a
        at = slice((p % 2) * part, (p % 2 + 1) * part)
        if p // 2:
            send_b[:, at] = b.astype(jnp.bfloat16)
        else:
            keep_b[:, at] = b


def close(sofar, own, oth, w_out, coef):
    ntok, width = sofar.shape
    keep = jax.ShapeDtypeStruct((ntok // 2, width // 2), jnp.float32)
    send = jax.ShapeDtypeStruct((ntok // 2, width // 2), jnp.bfloat16)
    return pl.pallas_call(
        close_kernel,
        in_specs=vmem(5),
        out_specs=vmem(4),
        out_shape=[keep, keep, send, send],
        compiler_params=params(16),
        cost_estimate=cost(4 * ntok * width * own.shape[1], 8 * ntok * width),
        name="close",
    )(sofar, own, oth, w_out, coef)


def neighbours(value, distance):
    count = lax.axis_size("seq")
    out = []
    for odd in (0, 1):
        lows = [i for i in range(count - distance) if (i // distance) % 2 == odd]
        route = [(i, i + distance) for i in lows] + [(i + distance, i) for i in lows]
        out.append(lax.ppermute(value, "seq", route))
    return out


def crossed(value, axis, bit):
    return lax.ppermute(value, axis, [(i, i ^ bit) for i in range(lax.axis_size(axis))])


def shards(
    hidden_states, modulation, w_query, w_key, w_value, w_out, block_ids, block_count, guidance
):
    _, ntok, model = hidden_states.shape
    tiles = block_ids.shape[0]
    width = w_query.shape[1]
    branch = lax.axis_index("guid")
    tp_here = lax.axis_index("tp")
    reach_dev = min(4, (lax.axis_size("seq") - 1) // 2)
    part = model // (2 * lax.axis_size("tp"))
    cut = int(width * FIRST_VALUES) // PAIR * PAIR
    modul = jnp.transpose(modulation, (1, 0, 2))

    h = norm(hidden_states, modul)

    def project(source, weight):
        return jnp.dot(source, weight, preferred_element_type=jnp.float32).astype(jnp.bfloat16)

    def near(value):
        out = [value]
        for distance in range(1, reach_dev + 1):
            out += neighbours(value, distance)
        return out

    key, h = lax.optimization_barrier((project(h, w_key), h))
    keys = near(key)
    value, h = lax.optimization_barrier((project(h, w_value), h))
    values = [near(value[:, :cut]), near(value[:, cut:])]
    query = project(h, w_query)

    there = (1 - branch) * (model // 2) + tp_here * part
    x_other = crossed(lax.dynamic_slice_in_dim(hidden_states[0], there, part, 1), "guid", 1)
    gate_other = crossed(modul[2:3], "guid", 1)
    query, x_other, gate_other = lax.optimization_barrier((query, x_other, gate_other))

    def finish(at, group, after):
        if reach_dev == 1:
            return gather(*weights, after, group, at.start // PAIR, tiles)
        return attend(block_ids, block_count, query[:, at], [k[:, at] for k in keys], group)

    if reach_dev == 1:
        span = (2 * tiles + 1) * (ntok // tiles)
        weights = weigh(block_ids, block_count, query, keys, span)
    first = finish(slice(0, cut), values[0], query)
    last = finish(slice(cut, width), values[1], first)
    sofar, coef = early(
        first, crossed(first, "guid", 1), w_out, hidden_states, x_other, modul, gate_other, guidance
    )
    keep_a, keep_b, send_a, send_b = close(sofar, last, crossed(last, "guid", 1), w_out, coef)
    got_a = crossed(send_a, "tp", 1)
    got_b = crossed(send_b, "tp", 2)
    sum_a = keep_a + got_a.astype(jnp.float32)
    sum_b = keep_b + got_b.astype(jnp.float32)
    last_a = crossed(sum_a[:, part:].astype(jnp.bfloat16), "tp", 2)
    last_b = crossed(sum_b[:, part:].astype(jnp.bfloat16), "tp", 1)
    return jnp.concatenate(
        [
            (sum_a[:, :part] + last_a.astype(jnp.float32)).astype(jnp.bfloat16),
            (sum_b[:, :part] + last_b.astype(jnp.float32)).astype(jnp.bfloat16),
        ],
        axis=0,
    )


def solution(mesh):
    in_specs = (
        P("guid", "seq", None),
        P("guid", None, None),
        P(None, "tp"),
        P(None, "tp"),
        P(None, "tp"),
        P("tp", None),
        P("seq", None),
        P("seq"),
        P(),
    )
    out_specs = P("seq", ("guid", "tp"))
    return jax.shard_map(shards, mesh=mesh, in_specs=in_specs, out_specs=out_specs, check_vma=False)
```

```python
import functools

import jax
import jax.numpy as jnp
from jax import lax
from jax.experimental import pallas as pl
from jax.experimental.pallas import tpu as pltpu
from jax.sharding import PartitionSpec as P

HD = 64
PAIR = 2 * HD
FIRST_VALUES = 8 / 12
NORM_ROWS = (1, 2, 3)
MIB = 1024 * 1024


def vmem(count):
    return [pl.BlockSpec(memory_space=pltpu.VMEM)] * count


def smem(count):
    return [pl.BlockSpec(memory_space=pltpu.SMEM)] * count


def params(mib):
    return pltpu.CompilerParams(vmem_limit_bytes=mib * MIB)


def cost(flops, nbytes, exps=0):
    return pl.CostEstimate(flops=int(flops), bytes_accessed=int(nbytes), transcendentals=int(exps))


def aligned(start, size):
    return pl.ds(pl.multiple_of(start, 128), size)


def norm_kernel(x_hbm, mod_hbm, h_ref, here_ref, there_ref, gate_ref, xb, mod_ref, sems):
    ntok, width = h_ref.shape
    rows = ntok // sum(NORM_ROWS)
    copies, starts, first = [], {}, 0
    for i, count in enumerate(NORM_ROWS):
        at = pl.ds(first * rows, count * rows)
        copies.append(pltpu.make_async_copy(x_hbm.at[0, at], xb.at[at], sems.at[i]))
        starts[first] = copies[-1]
        first += count
    copies.insert(1, pltpu.make_async_copy(mod_hbm, mod_ref, sems.at[len(NORM_ROWS)]))
    for copy in copies:
        copy.start()
    part = here_ref.shape[1]
    own = lax.axis_index("guid") * (width // 2) + lax.axis_index("tp") * part
    far = (1 - lax.axis_index("guid")) * (width // 2) + lax.axis_index("tp") * part
    for step in range(ntok // rows):
        if step in starts:
            starts[step].wait()
        at = slice(step * rows, (step + 1) * rows)
        xf = xb[at, :].astype(jnp.float32)
        cent = xf - jnp.mean(xf, axis=1, keepdims=True)
        var = jnp.mean(cent * cent, axis=1, keepdims=True)
        if step == 0:
            copies[1].wait()
            shift = mod_ref[0]
            scale = 1.0 + mod_ref[1]
            gate_ref[...] = mod_ref[2:3]
        h_ref[at, :] = (cent / jnp.sqrt(var + 1e-05) * scale + shift).astype(jnp.bfloat16)
    here_ref[...] = xb[:, aligned(own, part)]
    there_ref[...] = xb[:, aligned(far, part)]


def norm(states, modul, part):
    _, ntok, width = states.shape
    pinned = [pltpu.with_memory_space_constraint(one, pltpu.HBM) for one in (states, modul)]
    return pl.pallas_call(
        norm_kernel,
        in_specs=[pl.BlockSpec(memory_space=pl.ANY)] * 2,
        out_specs=vmem(4),
        out_shape=[
            jax.ShapeDtypeStruct((ntok, width), jnp.bfloat16),
            jax.ShapeDtypeStruct((ntok, part), jnp.bfloat16),
            jax.ShapeDtypeStruct((ntok, part), jnp.bfloat16),
            jax.ShapeDtypeStruct((1, 1, width), jnp.float32),
        ],
        scratch_shapes=[
            pltpu.VMEM((ntok, width), jnp.bfloat16),
            pltpu.VMEM((3, 1, width), jnp.float32),
            pltpu.SemaphoreType.DMA((len(NORM_ROWS) + 1,)),
        ],
        compiler_params=params(12),
        cost_estimate=cost(1e10, 4 * ntok * width, ntok),
        name="norm",
    )(*pinned)


def ahead_here(distance):
    return 1 - lax.rem(lax.div(lax.axis_index("seq"), distance), 2)


def spans_of(position, tiles, slots, trimmed):
    if not trimmed:
        return position, [(0, tiles)] * slots
    ahead, last = ahead_here(1), tiles - 1
    if position == 0:
        return last * ahead, [(0, tiles), (0, tiles), (last * ahead, 1)]
    if position == last:
        return last * (1 - ahead), [(0, tiles), (last * (1 - ahead), 1), (0, tiles)]
    if tiles - position == position + 1:
        count = position + 1
        return position, [(0, tiles), (position * (1 - ahead), count), (position * ahead, count)]
    return position, [(0, tiles)] * 3


def bias_rows(which, spans, tile_len, ids_ref, count_ref):
    here, tiles = lax.axis_index("seq"), ids_ref.shape[0]
    owners = [here]
    for distance in range(1, (len(spans) - 1) // 2 + 1):
        side = 2 * ahead_here(distance) - 1
        owners += [here + side * distance, here - side * distance]
    kmax = ids_ref.shape[1]
    live = count_ref[which]
    listed = [jnp.where(c < live, ids_ref[which, c], ids_ref[which, 0]) for c in range(kmax)]
    out = []
    for owner, (first, count) in zip(owners, spans):
        lane = lax.broadcasted_iota(jnp.int32, (1, count * tile_len), 1)
        tile = lax.div(lane, tile_len) + (owner * tiles + first)
        hit = functools.reduce(jnp.logical_or, [tile == one for one in listed])
        out.append(jnp.where(hit, 0.0, -1e30).astype(jnp.float32))
    return out


def score(q, keys, biases):
    lane = lax.broadcasted_iota(jnp.int32, q.shape, 1)
    q = q * jnp.asarray(0.125, q.dtype)
    zero = jnp.zeros_like(q)
    both = jnp.concatenate([jnp.where(lane < HD, q, zero), jnp.where(lane < HD, zero, q)], 0)
    return [
        lax.dot_general(both, k, (((1,), (1,)), ((), ())), preferred_element_type=jnp.float32) + b
        for k, b in zip(keys, biases)
    ]


def soften(scores):
    top = functools.reduce(jnp.maximum, [jnp.max(s, axis=1, keepdims=True) for s in scores])
    expo = [jnp.exp(s - top) for s in scores]
    total = sum(jnp.sum(e, axis=1, keepdims=True) for e in expo)
    return [e.astype(jnp.bfloat16) for e in expo], 1.0 / total


def by_head(stacked, width):
    half = stacked.shape[0] // 2
    lane = lax.broadcasted_iota(jnp.int32, (half, width), 1)
    return jnp.where(lane < HD, stacked[:half], stacked[half:])


def plan(tiles, tile_len, slots, trimmed, pairs):
    items = []
    for position in range(tiles):
        which, spans = spans_of(position, tiles, slots, trimmed)
        rows = pl.ds(pl.multiple_of(which * tile_len, tile_len), tile_len)
        keys = [pl.ds(pl.multiple_of(f * tile_len, tile_len), n * tile_len) for f, n in spans]
        items += [(position, which, spans, rows, keys, pair) for pair in range(pairs)]
    return items


def overlapped(items, begin, end):
    current = begin(items[0])
    for i, item in enumerate(items):
        following = begin(items[i + 1]) if i + 1 < len(items) else None
        end(item, current)
        current = following


def columns(pair):
    return slice(pair * PAIR, (pair + 1) * PAIR)


def weigh_kernel(tiles, trimmed, ids_ref, count_ref, q_ref, *refs):
    pieces, p_ref, inv_ref = refs[:-2], refs[-2], refs[-1]
    tile_len = q_ref.shape[0] // tiles
    pairs = q_ref.shape[1] // PAIR
    rows_of = {}

    def begin(item):
        position, which, spans, rows, keys, pair = item
        if position not in rows_of:
            rows_of[position] = bias_rows(which, spans, tile_len, ids_ref, count_ref)
        near = [piece[at, columns(pair)] for piece, at in zip(pieces, keys)]
        return score(q_ref[rows, columns(pair)], near, rows_of[position])

    def end(item, scores):
        position, which, spans, rows, keys, pair = item
        expo, inverse = soften(scores)
        slot, at = position * pairs + pair, 0
        for e in expo:
            p_ref[slot, :, at : at + e.shape[1]] = e
            at += e.shape[1]
        inv_ref[slot] = by_head(inverse, PAIR)

    overlapped(plan(tiles, tile_len, len(pieces), trimmed, pairs), begin, end)


def weigh(block_ids, block_count, query, pieces, span):
    ntok, width = query.shape
    tiles = block_ids.shape[0]
    items = tiles * width // PAIR
    tile_len = ntok // tiles
    return pl.pallas_call(
        functools.partial(weigh_kernel, tiles, True),
        in_specs=smem(2) + vmem(1 + len(pieces)),
        out_specs=vmem(2),
        out_shape=[
            jax.ShapeDtypeStruct((items, 2 * tile_len, span), jnp.bfloat16),
            jax.ShapeDtypeStruct((items, tile_len, PAIR), jnp.float32),
        ],
        compiler_params=params(24),
        cost_estimate=cost(0, 0),
        name="weigh",
    )(block_ids, block_count, query, *pieces)


def gather_kernel(tiles, first_pair, p_ref, inv_ref, _, *refs):
    pieces, o_ref = refs[:-1], refs[-1]
    tile_len = o_ref.shape[0] // tiles
    pairs = o_ref.shape[1] // PAIR
    all_pairs = p_ref.shape[0] // tiles
    for position, which, spans, rows, keys, pair in plan(tiles, tile_len, len(pieces), True, pairs):
        slot, start, acc = position * all_pairs + first_pair + pair, 0, 0.0
        for piece, at, (_, count) in zip(pieces, keys, spans):
            part = p_ref[slot, :, start : start + count * tile_len]
            acc += jnp.dot(part, piece[at, columns(pair)], preferred_element_type=jnp.float32)
            start += count * tile_len
        o_ref[rows, columns(pair)] = (by_head(acc, PAIR) * inv_ref[slot]).astype(jnp.bfloat16)


def gather(p, inv, after, pieces, first_pair, tiles, flops):
    ntok, width = pieces[0].shape
    return pl.pallas_call(
        functools.partial(gather_kernel, tiles, first_pair),
        in_specs=vmem(2) + [pl.BlockSpec(memory_space=pl.ANY)] + vmem(len(pieces)),
        out_specs=vmem(1)[0],
        out_shape=jax.ShapeDtypeStruct((ntok, width), jnp.bfloat16),
        compiler_params=params(24),
        cost_estimate=cost(flops, 0),
        name="gather",
    )(p, inv, after, *pieces)


def attend_kernel(tiles, slots, ids_ref, count_ref, q_ref, *refs):
    keys_refs, values, o_ref = refs[:slots], refs[slots : 2 * slots], refs[-1]
    tile_len = q_ref.shape[0] // tiles
    for position, which, spans, rows, keys, pair in plan(
        tiles, tile_len, slots, False, o_ref.shape[1] // PAIR
    ):
        biases = bias_rows(which, spans, tile_len, ids_ref, count_ref)
        near = [piece[at, columns(pair)] for piece, at in zip(keys_refs, keys)]
        expo, inverse = soften(score(q_ref[rows, columns(pair)], near, biases))
        acc = sum(
            jnp.dot(e, piece[at, columns(pair)], preferred_element_type=jnp.float32)
            for e, piece, at in zip(expo, values, keys)
        )
        o_ref[rows, columns(pair)] = by_head(acc * inverse, PAIR).astype(jnp.bfloat16)


def attend(block_ids, block_count, query, keys, values):
    ntok, width = query.shape
    span = ntok * len(keys)
    return pl.pallas_call(
        functools.partial(attend_kernel, block_ids.shape[0], len(keys)),
        in_specs=smem(2) + vmem(1 + 2 * len(keys)),
        out_specs=vmem(1)[0],
        out_shape=jax.ShapeDtypeStruct((ntok, width), jnp.bfloat16),
        compiler_params=params(40),
        cost_estimate=cost(8 * ntok * span * width, 4 * span * width, ntok * span * width / HD),
        name="attend",
    )(block_ids, block_count, query, *keys, *values)


def partner_starts(model, part):
    branch, here = lax.axis_index("guid"), lax.axis_index("tp")
    return [branch * (model // 2) + lax.bitwise_xor(here, p) * part for p in range(4)]


def early_kernel(own_ref, w_ref, x_ref, xo_ref, gate_ref, oth_gate_ref, scale_ref, y_ref, c_ref):
    part = x_ref.shape[1]
    starts = partner_starts(w_ref.shape[1], part)
    scale = scale_ref[0]
    branch = lax.axis_index("guid")
    mine = jnp.where(branch == 0, scale, 1.0 - scale)
    others = jnp.where(branch == 0, 1.0 - scale, scale)
    for p in range(4):
        at = aligned(starts[p], part)
        spot = slice(p * part, (p + 1) * part)
        gate = mine * gate_ref[0, :, at]
        c_ref[0:1, spot] = gate
        c_ref[1:2, spot] = others * oth_gate_ref[0, :, at]
        weight = w_ref[0 : own_ref.shape[1], at]
        y = gate * jnp.dot(own_ref[...], weight, preferred_element_type=jnp.float32)
        if p == 0:
            y += mine * x_ref[...].astype(jnp.float32) + others * xo_ref[...].astype(jnp.float32)
        y_ref[:, spot] = y


def early(own, w_out, x_own, x_other, gate_own, gate_other, scale):
    ntok, done = own.shape
    width, model = w_out.shape
    return pl.pallas_call(
        early_kernel,
        in_specs=vmem(6) + smem(1),
        out_specs=vmem(2),
        out_shape=[
            jax.ShapeDtypeStruct((ntok, model // 2), jnp.float32),
            jax.ShapeDtypeStruct((2, model // 2), jnp.float32),
        ],
        compiler_params=params(16),
        cost_estimate=cost(0, 0),
        name="early",
    )(own, w_out, x_own, x_other, gate_own, gate_other, scale)


def middle_kernel(early_ref, oth_ref, w_ref, c_ref, y_ref):
    part = early_ref.shape[1] // 4
    starts = partner_starts(w_ref.shape[1], part)
    for p in range(4):
        cols = slice(p * part, (p + 1) * part)
        weight = w_ref[0 : oth_ref.shape[1], aligned(starts[p], part)]
        added = jnp.dot(oth_ref[...], weight, preferred_element_type=jnp.float32)
        y_ref[:, cols] = early_ref[:, cols] + c_ref[1:2, cols] * added


def middle(sofar, oth, w_out, coef):
    return pl.pallas_call(
        middle_kernel,
        in_specs=vmem(4),
        out_specs=vmem(1)[0],
        out_shape=jax.ShapeDtypeStruct(sofar.shape, jnp.float32),
        compiler_params=params(16),
        cost_estimate=cost(2 * sofar.shape[0] * sofar.shape[1] * oth.shape[1], 0),
        name="middle",
    )(sofar, oth, w_out, coef)


def close_kernel(early_ref, own_ref, oth_ref, w_ref, c_ref, keep_a, keep_b, send_a, send_b):
    half = early_ref.shape[0] // 2
    part = early_ref.shape[1] // 4
    first = w_ref.shape[0] - own_ref.shape[1]
    starts = partner_starts(w_ref.shape[1], part)
    for p in (3, 1, 2, 0):
        cols = slice(p * part, (p + 1) * part)
        weight = w_ref[first:, aligned(starts[p], part)]
        y = early_ref[:, cols]
        y += c_ref[0:1, cols] * jnp.dot(own_ref[...], weight, preferred_element_type=jnp.float32)
        y += c_ref[1:2, cols] * jnp.dot(oth_ref[...], weight, preferred_element_type=jnp.float32)
        a, b = y[:half], y[half:]
        at = slice((p // 2) * part, (p // 2 + 1) * part)
        if p % 2:
            send_a[:, at] = a.astype(jnp.bfloat16)
        else:
            keep_a[:, at] = a
        at = slice((p % 2) * part, (p % 2 + 1) * part)
        if p // 2:
            send_b[:, at] = b.astype(jnp.bfloat16)
        else:
            keep_b[:, at] = b


def close(sofar, own, oth, w_out, coef):
    ntok, width = sofar.shape
    keep = jax.ShapeDtypeStruct((ntok // 2, width // 2), jnp.float32)
    send = jax.ShapeDtypeStruct((ntok // 2, width // 2), jnp.bfloat16)
    return pl.pallas_call(
        close_kernel,
        in_specs=vmem(5),
        out_specs=vmem(4),
        out_shape=[keep, keep, send, send],
        compiler_params=params(16),
        cost_estimate=cost(4 * ntok * width * own.shape[1], 8 * ntok * width),
        name="close",
    )(sofar, own, oth, w_out, coef)


def neighbours(value, distance):
    count = lax.axis_size("seq")
    out = []
    for odd in (0, 1):
        lows = [i for i in range(count - distance) if (i // distance) % 2 == odd]
        route = [(i, i + distance) for i in lows] + [(i + distance, i) for i in lows]
        out.append(lax.ppermute(value, "seq", route))
    return out


def crossed(value, axis, bit):
    return lax.ppermute(value, axis, [(i, i ^ bit) for i in range(lax.axis_size(axis))])


def shards(
    hidden_states, modulation, w_query, w_key, w_value, w_out, block_ids, block_count, guidance
):
    _, ntok, model = hidden_states.shape
    tiles = block_ids.shape[0]
    width = w_query.shape[1]
    reach_dev = min(4, (lax.axis_size("seq") - 1) // 2)
    part = model // (2 * lax.axis_size("tp"))
    cut = int(width * FIRST_VALUES) // PAIR * PAIR
    modul = jnp.transpose(modulation, (1, 0, 2))

    h, x_own, x_there, gate_own = norm(hidden_states, modul, part)

    def project(source, weight):
        return jnp.dot(source, weight, preferred_element_type=jnp.float32).astype(jnp.bfloat16)

    def near(value):
        out = [value]
        for distance in range(1, reach_dev + 1):
            out += neighbours(value, distance)
        return out

    key, h = lax.optimization_barrier((project(h, w_key), h))
    keys = near(key)
    value, query = lax.optimization_barrier((project(h, w_value), project(h, w_query)))
    values = [near(value[:, :cut]), near(value[:, cut:])]

    value, x_there, gate_own = lax.optimization_barrier((value, x_there, gate_own))
    x_other = crossed(x_there, "guid", 1)
    gate_other = crossed(gate_own, "guid", 1)
    query, x_other, gate_other = lax.optimization_barrier((query, x_other, gate_other))

    def finish(at, group, after):
        if reach_dev == 1:
            return gather(*weights, after, group, at.start // PAIR, tiles, 2e10 if at.start else 0)
        return attend(block_ids, block_count, query[:, at], [k[:, at] for k in keys], group)

    if reach_dev == 1:
        span = (2 * tiles + 1) * (ntok // tiles)
        weights = weigh(block_ids, block_count, query, keys, span)
    first = finish(slice(0, cut), values[0], query)
    sofar, coef = early(first, w_out, x_own, x_other, gate_own, gate_other, guidance)
    last = finish(slice(cut, width), values[1], coef)
    sofar = middle(sofar, crossed(first, "guid", 1), w_out, coef)
    keep_a, keep_b, send_a, send_b = close(sofar, last, crossed(last, "guid", 1), w_out, coef)
    got_a = crossed(send_a, "tp", 1)
    got_b = crossed(send_b, "tp", 2)
    sum_a = keep_a + got_a.astype(jnp.float32)
    sum_b = keep_b + got_b.astype(jnp.float32)
    last_a = crossed(sum_a[:, part:].astype(jnp.bfloat16), "tp", 2)
    last_b = crossed(sum_b[:, part:].astype(jnp.bfloat16), "tp", 1)
    return jnp.concatenate(
        [
            (sum_a[:, :part] + last_a.astype(jnp.float32)).astype(jnp.bfloat16),
            (sum_b[:, :part] + last_b.astype(jnp.float32)).astype(jnp.bfloat16),
        ],
        axis=0,
    )


def solution(mesh):
    in_specs = (
        P("guid", "seq", None),
        P("guid", None, None),
        P(None, "tp"),
        P(None, "tp"),
        P(None, "tp"),
        P("tp", None),
        P("seq", None),
        P("seq"),
        P(),
    )
    out_specs = P("seq", ("guid", "tp"))
    return jax.shard_map(shards, mesh=mesh, in_specs=in_specs, out_specs=out_specs, check_vma=False)
```
